32 devices in a mesh: section: 2 (over x), dp: 4 (over z), tensor: 4 (over y, core).
Axes of the slice: x: 2, y: 2, z: 4, core: 2. Of those that a mesh axis runs over, the one named last changes fastest.
Arguments:
- tokens_in: bfloat16 [2, 1024, 3072], P(None, ('dp', 'tensor')), parts along dimension 1, may hold values from -6 to 6
- norm_gains: float32 [2, 3072], P('section'), may hold values from 0.25 to 1.75
- w_gate: bfloat16 [2, 1, 3072, 1024], P('section', None, None, 'tensor'), may hold values from -0.109375 to 0.109375
- w_up: bfloat16 [2, 1, 3072, 1024], P('section', None, None, 'tensor'), may hold values from -0.109375 to 0.109375
- w_down: bfloat16 [2, 1, 1024, 3072], P('section', None, 'tensor'), may hold values from -0.1875 to 0.1875
- route_ids: int32 [2, 2, 1024, 2], P('section', None, 'dp'), parts along dimension 2, may hold values from 0 to 7, all different within a row; in each aligned block of 256 rows (0 to 255, 256 to 511, ..., all dimensions but the last counted through in order) at most 128 rows name the same one
- route_gates: float32 [2, 2, 1024, 2], P('section', None, 'dp'), parts along dimension 2, may hold values from 0.1 to 1
Outputs:
- layer_out: bfloat16 [2, 2, 1024, 3072], P('section', None, ('dp', 'tensor')), parts along dimension 2
The draws below stay inside these ranges and needn't reach their ends.
There are 4 independent parts, one for each index of `dp`. The reference program is written for one: setup_inputs(seed, part) draws one part's arguments, and reference() takes and returns one part's arrays. A program takes and returns all parts, laid end to end along the dimension named above; an argument that names none is the same for every part. Nothing has to cross between parts.
Inputs may be any that keep to these rules, and one draw needn't show every extreme that they name: `route_ids`: each token names two different experts; in each micro-batch of 256 tokens of one layer no expert is named by more than 128 tokens, a bound that some block reaches.
All inputs are finite; a program needn't handle non-finite values.
Results may differ from the reference program's by a relative error of at most 0.0055.
Values may be sent and summed in bfloat16 or wider, within the bound.
A program may use at most 64 MiB of HBM per device.

```python
import math
import jax
import jax.numpy as jnp
import numpy as np
from jax import lax

D = 3072
EXPERTS = 8
EXP_WIN = 1
HID_DEV = 256
MB = 2
TOK = 256
CAP = 128
HIDDEN_SIZE = 1024
N_TENSOR = 4


def block_levels(key, extent, split, low, top_value):
    loudness = 1.0
    for dim, blocks in split:
        steps = jax.random.uniform(jax.random.fold_in(jax.random.fold_in(key, 6), dim), (blocks,), jnp.float32, low / len(split), top_value / len(split))
        loudness = loudness * jnp.repeat(jnp.exp(steps), extent[dim] // blocks).reshape((-1,) + (1,) * (len(extent) - 1 - dim))
    return loudness


def deal_out(stream_key, own, number, rows, amount, top, bound, slope):
    order = jax.random.permutation(stream_key, amount)
    crowded, common = load_shares(amount, rows * top, bound, slope, True), load_shares(amount, rows * top, bound, slope, False)
    places = jnp.arange(amount)

    def named(lengths, turn):
        used = int((lengths > 0).sum())
        fixed = max(1, used // 4)
        shifted = fixed + (places - fixed + turn * (used - fixed)) % max(1, amount - fixed)
        return jnp.zeros((amount,), jnp.int32).at[order[jnp.where(places < fixed, places, shifted)]].set(jnp.asarray(lengths, jnp.int32))

    lengths = jnp.where(number % 4 == 0, named(crowded, number // 4), named(common, number - number // 4 - 1))
    mixed = jax.random.permutation(jax.random.fold_in(own, 3), amount)
    giver, sink = mixed[0:amount // 2 * 2:2], mixed[1:amount // 2 * 2:2]
    slack = jnp.minimum(lengths[giver] - 1, bound - lengths[sink]) // 2
    slack = jnp.where((giver == order[0]) | (sink == order[0]) | (lengths[sink] == 0), 0, jnp.maximum(slack, 0))
    shifted = jax.random.randint(jax.random.fold_in(own, 4), (amount // 2,), 0, 1 << 20) % (slack + 1)
    lengths = lengths.at[giver].add(-shifted).at[sink].add(shifted)
    members = jnp.searchsorted(jnp.cumsum(lengths), jnp.arange(rows * top), side="right").astype(jnp.int32)
    grid = members.reshape(top, rows).T
    grid = grid[jax.random.permutation(jax.random.fold_in(own, 1), rows)]
    turn = jax.random.randint(jax.random.fold_in(own, 2), (rows, 1), 0, top)
    return jnp.take_along_axis(grid, (jnp.arange(top)[None, :] + turn) % top, axis=1)


def load_shares(number_of, total, reach, slope, full):
    weights = [(1 << 20) // math.isqrt(standing ** slope) + 1 for standing in range(1, number_of + 1)]
    largest = reach if full else min(reach, max(-(-total // number_of), total * weights[0] // sum(weights)))
    least = 1 if total - largest >= number_of - 1 else 0
    counts, spare = [largest] + [least] * (number_of - 1), total - largest - least * (number_of - 1)
    while spare > 0:
        free = [i for i in range(1, number_of) if counts[i] < largest] or [i for i in range(1, number_of) if counts[i] < reach]
        whole, budget = sum([weights[i] for i in free]), spare
        for i in free:
            more = min(reach - counts[i], max(1, budget * weights[i] // whole), spare)
            counts[i] = counts[i] + more
            spare = spare - more
    return np.array(counts)


def bell_draw(own_key, extent, scale, reach, cuts=(), dtype=jnp.bfloat16):
    array = scale * jax.random.normal(own_key, extent, jnp.float32)
    if cuts:
        array = array * block_levels(own_key, extent, cuts, -0.22, 0.18)
    return jnp.clip(array, -reach, reach).astype(dtype)


def setup_inputs(seed: int = 0, part: int = 0) -> dict:
    keys = jax.random.split(jax.random.key(seed), 8)
    part_keys = jax.random.split(jax.random.fold_in(keys[7], part), 8)
    tokens_in = bell_draw(part_keys[0], (MB, TOK, D), 1.0, 6.0, ((1, 4),))
    norm_gains = jnp.clip(1.0 + 0.15 * jax.random.normal(keys[1], (2, D), jnp.float32), 0.25, 1.75)
    w_gate = bell_draw(keys[2], (2, EXP_WIN, D, HIDDEN_SIZE), D ** -0.5, 0.109375, ((0, 2), (3, 4)))
    w_up = bell_draw(keys[3], (2, EXP_WIN, D, HIDDEN_SIZE), D ** -0.5, 0.109375, ((0, 2), (3, 4)))
    w_down = bell_draw(keys[4], (2, EXP_WIN, HIDDEN_SIZE, D), HIDDEN_SIZE ** -0.5, 0.1875, ((0, 2), (2, 4)))
    route_ids_keys = jax.random.split(jax.random.fold_in(part_keys[5], 1), 2 * MB * TOK // TOK)
    route_ids_turns = jax.random.permutation(jax.random.fold_in(part_keys[5], 3), 2 * MB * TOK // TOK)
    route_ids = jax.vmap(lambda own, number: deal_out(jax.random.fold_in(part_keys[5], 2), own, number, TOK, EXPERTS, 2, CAP, 1))(route_ids_keys, route_ids_turns).reshape((2, MB, TOK, 2))
    route_gates = jnp.clip(0.1 + 0.9 * jax.random.uniform(part_keys[6], (2, MB, TOK, 2), jnp.float32) ** block_levels(part_keys[6], (2, MB, TOK, 2), ((0, 2),), -0.2, 0.2), 0.1, 1.0)
    return {"tokens_in": tokens_in, "norm_gains": norm_gains, "w_gate": w_gate, "w_up": w_up, "w_down": w_down, "route_ids": route_ids, "route_gates": route_gates}


def normalize(rows, gain_row):
    values = rows.astype(jnp.float32)
    scale = lax.rsqrt(lax.optimization_barrier(jnp.mean(values * values, axis=-1, keepdims=True)) + 1e-05)
    return (values * scale * gain_row).astype(jnp.bfloat16)

def expert_partial(whole_rows, gate_part, up_part, down_part, ids_now, gates_now):
    total = jnp.zeros((whole_rows.shape[0], whole_rows.shape[1]), jnp.float32)
    for e in range(gate_part.shape[0]):
        picked = ids_now == e
        chosen = lax.optimization_barrier(jnp.sum(picked.astype(jnp.int32), axis=-1))
        weight = lax.optimization_barrier(jnp.sum(jnp.where(picked, gates_now, 0.0), axis=-1))
        slot = jnp.cumsum(chosen) - 1
        positions = lax.broadcasted_iota(jnp.int32, (CAP, whole_rows.shape[0]), 0)
        select = ((slot[None, :] == positions) & (chosen[None, :] > 0)).astype(jnp.bfloat16)
        block = jnp.dot(select, whole_rows, preferred_element_type=jnp.float32).astype(jnp.bfloat16)
        gate_val = jnp.dot(block, gate_part[e], preferred_element_type=jnp.float32)
        up_val = jnp.dot(block, up_part[e], preferred_element_type=jnp.float32)
        act = (jax.nn.silu(gate_val) * up_val).astype(jnp.bfloat16)
        result = jnp.dot(act, down_part[e], preferred_element_type=jnp.float32)
        back = jnp.take(result, jnp.clip(slot, 0, CAP - 1).astype(jnp.int32), axis=0)
        total = total + back * weight[:, None]
    return total

def layer(rows, gain_row, gate_w, up_w, down_w, ids_now, gates_now):
    normed = normalize(rows, gain_row)
    width = gate_w.shape[1]
    gate_split = gate_w.reshape(EXP_WIN, width, N_TENSOR, HID_DEV).transpose(2, 0, 1, 3)
    up_split = up_w.reshape(EXP_WIN, width, N_TENSOR, HID_DEV).transpose(2, 0, 1, 3)
    down_split = down_w.reshape(EXP_WIN, N_TENSOR, HID_DEV, width).transpose(1, 0, 2, 3)

    def shard_term(pieces):
        partial_value = expert_partial(normed, pieces[0], pieces[1], pieces[2], ids_now, gates_now)
        return partial_value.astype(jnp.bfloat16)
    terms = lax.map(shard_term, (gate_split, up_split, down_split))
    summed = lax.optimization_barrier(jnp.sum(lax.optimization_barrier(terms).astype(jnp.float32), axis=0))
    return (rows.astype(jnp.float32) + summed).astype(jnp.bfloat16)

def reference(tokens_in, norm_gains, w_gate, w_up, w_down, route_ids, route_gates):
    firsts = []
    seconds = []
    for m in range(MB):
        first_out = layer(tokens_in[m], norm_gains[0], w_gate[0], w_up[0], w_down[0], route_ids[0, m], route_gates[0, m])
        second_out = layer(first_out, norm_gains[1], w_gate[1], w_up[1], w_down[1], route_ids[1, m], route_gates[1, m])
        firsts.append(first_out)
        seconds.append(second_out)
    return jnp.stack([jnp.stack(firsts), jnp.stack(seconds)])
```

```python
import functools

import jax
import jax.numpy as jnp
from jax import lax
from jax.experimental import pallas as pl
from jax.experimental.pallas import tpu as pltpu
from jax.sharding import PartitionSpec as P

CAP = 128
HALF = CAP // 2
MESH = pl.DeviceIdType.MESH
F32 = jnp.float32
BF16 = jnp.bfloat16


def dot_nt(a, b):
    return lax.dot_general(a, b, (((1,), (1,)), ((), ())), preferred_element_type=F32)


def kernel(
    n, micro, tok_ref, gain_ref, route_ref, wg_hbm, wu_hbm, wd_hbm, out_ref,
    rows, wg, wu, wd, peer_route, blocks, term, from_mate, chip_sum, from_chip, sums, own_rows, result,
    tok_sem, w_sem, out_sem, route_sems,
    g_send, g_recv, f_send, a_send, a_recv, b_send, b_recv, c_send, c_recv, d_send, d_recv, e_send, e_recv,
):
    chips = n // 2
    rpd = tok_ref.shape[1]
    width = tok_ref.shape[2]
    tok = n * rpd
    cols = width // chips
    sec = lax.axis_index("section")
    me = lax.axis_index("tensor")
    chip = me // 2
    core = me % 2
    mate = chip * 2 + (1 - core)
    other = 1 - sec
    sends = []

    def chip_at(step):
        return lax.rem(chip + step, chips)

    def remote(src, dst, send, recv, **where):
        return pltpu.make_async_remote_copy(
            src_ref=src, dst_ref=dst, send_sem=send, recv_sem=recv, device_id=where, device_id_type=MESH
        )

    def rows_of(index):
        return pl.ds(pl.multiple_of(index * rpd, rpd), rpd)

    my_half = pl.ds(pl.multiple_of(core * HALF, HALF), HALF)
    mate_half = pl.ds(pl.multiple_of((1 - core) * HALF, HALF), HALF)

    def own_copy(m):
        return pltpu.make_async_copy(tok_ref.at[m], rows.at[m, rows_of(me), :], tok_sem.at[m])

    def weight_copies():
        pairs = ((wg_hbm, wg), (wu_hbm, wu), (wd_hbm, wd))
        return [pltpu.make_async_copy(src, dst, w_sem.at[i]) for i, (src, dst) in enumerate(pairs)]

    for m in range(micro):
        own_copy(m).start()
    for copy in weight_copies():
        copy.start()

    barrier = pltpu.get_barrier_semaphore()
    for step in range(1, chips):
        pl.semaphore_signal(barrier, inc=1, device_id={"tensor": chip_at(step) * 2 + core}, device_id_type=MESH)
    pl.semaphore_signal(barrier, inc=1, device_id={"tensor": mate}, device_id_type=MESH)
    pl.semaphore_signal(barrier, inc=1, device_id={"section": other}, device_id_type=MESH)
    pl.semaphore_wait(barrier, chips + 1)

    def gather(m, owner, target, from_tokens, send):
        place = rows.at[m, rows_of(owner), :]
        return remote(tok_ref.at[m] if from_tokens else place, place, send, g_recv.at[m, owner], tensor=target)

    first = []

    def route_copy():
        return remote(route_ref, peer_route, route_sems.at[0], route_sems.at[1], section=other)

    route_copy().start()
    first.append(route_copy())
    for m in range(micro):
        for step in range(1, chips):
            copy = gather(m, me, chip_at(step) * 2 + core, True, g_send.at[m, step])
            copy.start()
            first.append(copy)
        copy = gather(m, me, mate, True, g_send.at[m, 0])
        copy.start()
        first.append(copy)

    def forward(m):
        for step in range(1, chips):
            owner = chip_at(step) * 2 + core
            copy = gather(m, owner, mate, False, f_send.at[m, step])
            copy.wait_recv()
            copy.start()
            sends.append(copy)

    def gathered(m):
        own_copy(m).wait()
        for step in range(chips):
            owner = chip_at(step) * 2 + (1 - core)
            gather(m, owner, mate, False, f_send.at[m, step]).wait_recv()

    tri = (
        lax.broadcasted_iota(jnp.int32, (tok, tok), 0) <= lax.broadcasted_iota(jnp.int32, (tok, tok), 1)
    ).astype(F32).astype(BF16)

    def selection(ref, m):
        chosen = ref[m : m + 1, :]
        counts = jnp.dot(jnp.broadcast_to(chosen, (16, tok)).astype(BF16), tri, preferred_element_type=F32)
        slot = (counts[0:1, :] - 1.0).astype(jnp.int32)
        hit = (slot == lax.broadcasted_iota(jnp.int32, (CAP, tok), 0)) & (chosen > 0.5)
        return jnp.where(hit, 1.0, 0.0)

    def mine(select):
        pick = lax.broadcasted_iota(jnp.int32, (rpd, tok), 1) == lax.broadcasted_iota(
            jnp.int32, (rpd, tok), 0
        ) + me * rpd
        return dot_nt(pick.astype(F32).astype(BF16), select).astype(BF16)

    def take(m, select):
        for k in range(chips):
            at = pl.ds(k * cols, cols)
            blocks[m, :, at] = jnp.dot(select, rows[m, :, at], preferred_element_type=F32)

    def experts(m, select):
        weight = jnp.sum(select * route_ref[micro + m : micro + m + 1, :], axis=1, keepdims=True)
        block = blocks[m]
        scale = lax.rsqrt(jnp.mean(block * block, axis=1, keepdims=True) + 1e-05)
        normed = (block * scale * gain_ref[...]).astype(BF16)
        gate = jnp.dot(normed, wg[...], preferred_element_type=F32)
        up = jnp.dot(normed, wu[...], preferred_element_type=F32)
        act = (gate / (1.0 + jnp.exp(-gate)) * up).astype(BF16)
        for k in range(chips):
            part = jnp.dot(act, wd[:, k * cols : (k + 1) * cols], preferred_element_type=F32)
            term[m, k] = (part * weight).astype(BF16)
        copy = to_mate(m)
        copy.start()
        sends.append(copy)

    def to_mate(m):
        return remote(term.at[m, :, mate_half, :], from_mate.at[m], a_send.at[m], a_recv.at[m], tensor=mate)

    def to_chip(m, step):
        there = chip_at(step)
        return remote(
            chip_sum.at[m, there], from_chip.at[m, step], b_send.at[m, step], b_recv.at[m, step],
            tensor=there * 2 + core,
        )

    def piece(layer, m, k, half):
        return sums.at[layer, m, k, half, :]

    def to_section(m):
        place = piece(0, m, chip, my_half)
        return remote(place, place, c_send.at[m], c_recv.at[m], section=other)

    def spread(layer, m, step):
        place = piece(layer, m, chip, my_half)
        return remote(
            place, place, d_send.at[layer, m, step], d_recv.at[layer, m, step], tensor=chip_at(step) * 2 + core
        )

    def share(layer, m, step, half):
        place = piece(layer, m, chip_at(step), half)
        return remote(place, place, e_send.at[layer, m, step], e_recv.at[layer, m, step], tensor=mate)

    def go(copy):
        copy.start()
        sends.append(copy)

    def reduce_core(m):
        to_mate(m).wait_recv()
        for k in range(chips):
            chip_sum[m, k] = (term[m, k, my_half, :].astype(F32) + from_mate[m, k].astype(F32)).astype(BF16)
        for step in range(1, chips):
            go(to_chip(m, step))

    def reduce_chip(layer, m):
        total = chip_sum[m, chip].astype(F32)
        for step in range(1, chips):
            to_chip(m, step).wait_recv()
            total = total + from_chip[m, step].astype(F32)
        sums[layer, m, chip, my_half, :] = total.astype(BF16)

    def start_spread(layer, m):
        for step in range(1, chips):
            go(spread(layer, m, step))
        go(share(layer, m, 0, my_half))

    def finish_spread(layer, m):
        for step in range(1, chips):
            spread(layer, m, step).wait_recv()
        for step in range(1, chips):
            go(share(layer, m, step, my_half))

    def spread_done(layer, m):
        for step in range(chips):
            share(layer, m, step, mate_half).wait_recv()

    def out_copy(m):
        return pltpu.make_async_copy(result.at[m], out_ref.at[m], out_sem.at[m])

    def add_own(layer, m, source, select_own, target):
        for k in range(chips):
            at = pl.ds(k * cols, cols)
            more = jnp.dot(select_own, sums[layer, m, k], preferred_element_type=F32)
            target[m, :, at] = (source[:, at].astype(F32) + more).astype(BF16)

    def wait_sends():
        for copy in sends:
            copy.wait_send()
        sends.clear()

    @pl.when(sec == 0)
    def _():
        selects = [selection(route_ref, m) for m in range(micro)]
        for copy in weight_copies():
            copy.wait()
        forward(0)
        gathered(0)
        take(0, selects[0].astype(BF16))
        experts(0, selects[0])
        forward(1)
        reduce_core(0)
        gathered(1)
        take(1, selects[1].astype(BF16))
        experts(1, selects[1])
        reduce_chip(0, 0)
        go(to_section(0))
        start_spread(0, 0)
        reduce_core(1)
        finish_spread(0, 0)
        reduce_chip(0, 1)
        go(to_section(1))
        start_spread(0, 1)
        for m in range(micro):
            if m == 1:
                finish_spread(0, 1)
            spread_done(0, m)
            add_own(0, m, rows.at[m, rows_of(me), :], mine(selects[m].astype(BF16)), result)
            out_copy(m).start()
        route_copy().wait_recv()
        wait_sends()
        for m in range(micro):
            out_copy(m).wait()

    @pl.when(sec == 1)
    def _():
        selects = [selection(route_ref, m) for m in range(micro)]
        for copy in weight_copies():
            copy.wait()
        route_copy().wait_recv()
        before = [selection(peer_route, m).astype(BF16) for m in range(micro)]
        for m in range(micro):
            forward(m)
            gathered(m)
            take(m, selects[m].astype(BF16))

        def second(m):
            spread_done(0, m)
            link = dot_nt(selects[m].astype(BF16), before[m]).astype(BF16)
            for k in range(chips):
                at = pl.ds(k * cols, cols)
                more = jnp.dot(link, sums[0, m, k], preferred_element_type=F32)
                blocks[m, :, at] = (blocks[m, :, at] + more).astype(BF16).astype(F32)
            experts(m, selects[m])
            add_own(0, m, rows.at[m, rows_of(me), :], mine(before[m]), own_rows)

        to_section(0).wait_recv()
        start_spread(0, 0)
        finish_spread(0, 0)
        second(0)
        to_section(1).wait_recv()
        start_spread(0, 1)
        reduce_core(0)
        finish_spread(0, 1)
        second(1)
        reduce_chip(1, 0)
        start_spread(1, 0)
        reduce_core(1)
        finish_spread(1, 0)
        reduce_chip(1, 1)
        start_spread(1, 1)
        for m in range(micro):
            if m == 1:
                finish_spread(1, 1)
            spread_done(1, m)
            add_own(1, m, own_rows.at[m], mine(selects[m].astype(BF16)), result)
            out_copy(m).start()
        wait_sends()
        for m in range(micro):
            out_copy(m).wait()

    for copy in first:
        copy.wait_send()


def body(tokens_in, norm_gains, w_gate, w_up, w_down, route_ids, route_gates):
    n = lax.axis_size("tensor")
    micro, rpd, width = tokens_in.shape
    chips = n // 2
    cols = width // chips
    tok = n * rpd
    hidden = w_gate.shape[-1]
    picked = route_ids[0] == 0
    chosen = jnp.sum(picked.astype(F32), axis=-1)
    weight = jnp.sum(jnp.where(picked, route_gates[0], 0.0), axis=-1)
    route = jnp.concatenate([chosen, weight, jnp.zeros((8 - 2 * micro, tok), F32)], axis=0)
    dma = pltpu.SemaphoreType.DMA
    out = pl.pallas_call(
        functools.partial(kernel, n, micro),
        out_shape=jax.ShapeDtypeStruct((micro, rpd, width), BF16),
        in_specs=[
            pl.BlockSpec(memory_space=pl.ANY),
            pl.BlockSpec(memory_space=pltpu.VMEM),
            pl.BlockSpec(memory_space=pltpu.VMEM),
            pl.BlockSpec(memory_space=pl.ANY),
            pl.BlockSpec(memory_space=pl.ANY),
            pl.BlockSpec(memory_space=pl.ANY),
        ],
        out_specs=pl.BlockSpec(memory_space=pl.ANY),
        scratch_shapes=[
            pltpu.VMEM((micro, tok, width), BF16),
            pltpu.VMEM((width, hidden), BF16),
            pltpu.VMEM((width, hidden), BF16),
            pltpu.VMEM((hidden, width), BF16),
            pltpu.VMEM((8, tok), F32),
            pltpu.VMEM((micro, CAP, width), F32),
            pltpu.VMEM((micro, chips, CAP, cols), BF16),
            pltpu.VMEM((micro, chips, HALF, cols), BF16),
            pltpu.VMEM((micro, chips, HALF, cols), BF16),
            pltpu.VMEM((micro, chips, HALF, cols), BF16),
            pltpu.VMEM((2, micro, chips, CAP, cols), BF16),
            pltpu.VMEM((micro, rpd, width), BF16),
            pltpu.VMEM((micro, rpd, width), BF16),
            dma((micro,)),
            dma((3,)),
            dma((micro,)),
            dma((2,)),
            dma((micro, chips)),
            dma((micro, n)),
            dma((micro, chips)),
            dma((micro,)),
            dma((micro,)),
            dma((micro, chips)),
            dma((micro, chips)),
            dma((micro,)),
            dma((micro,)),
            dma((2, micro, chips)),
            dma((2, micro, chips)),
            dma((2, micro, chips)),
            dma((2, micro, chips)),
        ],
        compiler_params=pltpu.CompilerParams(
            collective_id=0, has_side_effects=True, vmem_limit_bytes=48 * 1024 * 1024
        ),
        cost_estimate=pl.CostEstimate(flops=2 * 10**9, bytes_accessed=8 * 10**6, transcendentals=10**5),
        name="relay",
    )(tokens_in, norm_gains, route, w_gate[0, 0], w_up[0, 0], w_down[0, 0])
    return out[None]


def solution(mesh):
    return jax.shard_map(
        body,
        mesh=mesh,
        in_specs=(
            P(None, ("dp", "tensor"), None),
            P("section", None),
            P("section", None, None, "tensor"),
            P("section", None, None, "tensor"),
            P("section", None, "tensor", None),
            P("section", None, "dp", None),
            P("section", None, "dp", None),
        ),
        out_specs=P("section", None, ("dp", "tensor"), None),
        check_vma=False,
    )
```

```python
import functools

import jax
import jax.numpy as jnp
from jax import lax
from jax.experimental import pallas as pl
from jax.experimental.pallas import tpu as pltpu
from jax.sharding import PartitionSpec as P

CAP = 128
HALF = CAP // 2
PIECES = 4
STRIP = HALF // PIECES
SPLIT = 2
MESH = pl.DeviceIdType.MESH
F32 = jnp.float32
BF16 = jnp.bfloat16


def dot_nt(a, b):
    return lax.dot_general(a, b, (((1,), (1,)), ((), ())), preferred_element_type=F32)


def kernel(
    n, micro, tok_ref, gain_ref, route_ref, wg_hbm, wu_hbm, wd_hbm, out_ref,
    rows, wg, wu, wd, peer_route, blocks, term, from_mate, chip_sum, from_chip, sums, own_rows, result,
    tok_sem, w_sem, out_sem, route_sems,
    g_send, g_recv, y_send, y_recv, x_send, x_recv, fy_send, fy_recv, fx_send, fx_recv, a_send, a_recv, b_send, b_recv, c_send, c_recv, d_send, d_recv, e_send, e_recv,
):
    chips = n // 2
    rpd = tok_ref.shape[1]
    width = tok_ref.shape[2]
    tok = n * rpd
    cols = width // chips
    sec = lax.axis_index("section")
    me = lax.axis_index("tensor")
    chip = me // 2
    core = me % 2
    mate = chip * 2 + (1 - core)
    other = 1 - sec
    sends = []

    def chip_at(step):
        return lax.rem(chip + step, chips)

    def remote(src, dst, send, recv, **where):
        return pltpu.make_async_remote_copy(
            src_ref=src, dst_ref=dst, send_sem=send, recv_sem=recv, device_id=where, device_id_type=MESH
        )

    def rows_of(index):
        return pl.ds(pl.multiple_of(index * rpd, rpd), rpd)

    my_half = pl.ds(pl.multiple_of(core * HALF, HALF), HALF)
    mate_half = pl.ds(pl.multiple_of((1 - core) * HALF, HALF), HALF)

    def own_copy(m):
        return pltpu.make_async_copy(tok_ref.at[m], rows.at[m, rows_of(me), :], tok_sem.at[m])

    def weight_copies():
        pairs = ((wg_hbm, wg), (wu_hbm, wu), (wd_hbm, wd))
        return [pltpu.make_async_copy(src, dst, w_sem.at[i]) for i, (src, dst) in enumerate(pairs)]

    for m in range(micro):
        own_copy(m).start()
    for copy in weight_copies():
        copy.start()

    barrier = pltpu.get_barrier_semaphore()
    for step in range(1, chips):
        pl.semaphore_signal(barrier, inc=1, device_id={"tensor": chip_at(step) * 2 + core}, device_id_type=MESH)
    pl.semaphore_signal(barrier, inc=1, device_id={"tensor": mate}, device_id_type=MESH)
    pl.semaphore_signal(barrier, inc=1, device_id={"section": other}, device_id_type=MESH)
    pl.semaphore_wait(barrier, chips + 1)

    span = width // 2 // SPLIT

    def route_copy():
        return remote(route_ref, peer_route, route_sems.at[0], route_sems.at[1], section=other)

    def lanes_of(section, i):
        return pl.ds(pl.multiple_of(section * (width // 2) + i * span, 128), span)

    def own_to_mate(m):
        return remote(tok_ref.at[m], rows.at[m, rows_of(me), :], g_send.at[m], g_recv.at[m], tensor=mate)

    def over_chips(m, step, i):
        lanes = lanes_of(sec, i)
        return remote(
            tok_ref.at[m, :, lanes], rows.at[m, rows_of(me), lanes], y_send.at[m, step, i], y_recv.at[m, step, i],
            tensor=chip_at(step) * 2 + core,
        )

    def from_step(step):
        return chip_at(chips - step) * 2 + core

    def over_sections(m, step, i):
        place = rows.at[m, rows_of(from_step(step)), lanes_of(sec, i)]
        return remote(place, place, x_send.at[m, step, i], x_recv.at[m, step, i], section=other)

    def pass_own(m, step, i):
        place = rows.at[m, rows_of(from_step(step)), lanes_of(sec, i)]
        return remote(place, place, fy_send.at[m, step, i], fy_recv.at[m, step, i], tensor=mate)

    def pass_other(m, step, i):
        place = rows.at[m, rows_of(from_step(step)), lanes_of(other, i)]
        return remote(place, place, fx_send.at[m, step, i], fx_recv.at[m, step, i], tensor=mate)

    hops = [(step, i) for step in range(1, chips) for i in range(SPLIT)]
    first = []
    for m in range(micro):
        for step, i in hops:
            over_chips(m, step, i).start()
            first.append(over_chips(m, step, i))
        own_to_mate(m).start()
        first.append(own_to_mate(m))
        if m == 0:
            route_copy().start()
            first.append(route_copy())

    def forward(m):
        for step, i in hops:
            over_chips(m, step, i).wait_recv()
            go(over_sections(m, step, i))
            go(pass_own(m, step, i))

    def forward_other(m):
        for step, i in hops:
            over_sections(m, step, i).wait_recv()
            go(pass_other(m, step, i))

    def gathered(m):
        own_copy(m).wait()
        own_to_mate(m).wait_recv()
        for step, i in hops:
            pass_own(m, step, i).wait_recv()
            pass_other(m, step, i).wait_recv()

    tri = (
        lax.broadcasted_iota(jnp.int32, (tok, tok), 0) <= lax.broadcasted_iota(jnp.int32, (tok, tok), 1)
    ).astype(F32).astype(BF16)

    def selection(ref, m):
        chosen = ref[m : m + 1, :]
        counts = jnp.dot(jnp.broadcast_to(chosen, (16, tok)).astype(BF16), tri, preferred_element_type=F32)
        slot = (counts[0:1, :] - 1.0).astype(jnp.int32)
        hit = (slot == lax.broadcasted_iota(jnp.int32, (CAP, tok), 0)) & (chosen > 0.5)
        return jnp.where(hit, 1.0, 0.0)

    def mine(select):
        pick = lax.broadcasted_iota(jnp.int32, (rpd, tok), 1) == lax.broadcasted_iota(
            jnp.int32, (rpd, tok), 0
        ) + me * rpd
        return dot_nt(pick.astype(F32).astype(BF16), select).astype(BF16)

    def take(m, select):
        for k in range(chips):
            at = pl.ds(k * cols, cols)
            blocks[m, :, at] = jnp.dot(select, rows[m, :, at], preferred_element_type=F32)

    def experts(m, select):
        weight = jnp.sum(select * route_ref[micro + m : micro + m + 1, :], axis=1, keepdims=True)
        block = blocks[m]
        scale = lax.rsqrt(jnp.mean(block * block, axis=1, keepdims=True) + 1e-05)
        normed = (block * scale * gain_ref[...]).astype(BF16)
        gate = jnp.dot(normed, wg[...], preferred_element_type=F32)
        up = jnp.dot(normed, wu[...], preferred_element_type=F32)
        act = (gate / (1.0 + jnp.exp(-gate)) * up).astype(BF16)
        for k in range(chips):
            part = jnp.dot(act, wd[:, k * cols : (k + 1) * cols], preferred_element_type=F32)
            term[m, k] = (part * weight).astype(BF16)
        copy = to_mate(m)
        copy.start()
        sends.append(copy)

    def to_mate(m):
        return remote(term.at[m, :, mate_half, :], from_mate.at[m], a_send.at[m], a_recv.at[m], tensor=mate)

    def strip(base, p):
        return pl.ds(pl.multiple_of(base * HALF + p * STRIP, STRIP), STRIP)

    def to_chip(m, step, p):
        there = chip_at(step)
        at = pl.ds(p * STRIP, STRIP)
        return remote(
            chip_sum.at[m, there, at, :], from_chip.at[m, step, at, :], b_send.at[m, step, p], b_recv.at[m, step, p],
            tensor=there * 2 + core,
        )

    def to_section(m, p):
        place = sums.at[0, m, chip, strip(core, p), :]
        return remote(place, place, c_send.at[m, p], c_recv.at[m, p], section=other)

    def spread(layer, m, step, p):
        place = sums.at[layer, m, chip, strip(core, p), :]
        return remote(
            place, place, d_send.at[layer, m, step, p], d_recv.at[layer, m, step, p], tensor=chip_at(step) * 2 + core
        )

    def share(layer, m, step, p):
        place = sums.at[layer, m, chip_at(chips - step), strip(core, p), :]
        return remote(place, place, e_send.at[layer, m, step, p], e_recv.at[layer, m, step, p], tensor=mate)

    def go(copy):
        copy.start()
        sends.append(copy)

    def reduce_core(m):
        to_mate(m).wait_recv()
        for k in range(chips):
            chip_sum[m, k] = (term[m, k, my_half, :].astype(F32) + from_mate[m, k].astype(F32)).astype(BF16)
        for p in range(PIECES):
            for step in range(1, chips):
                go(to_chip(m, step, p))

    def reduce_chip(layer, m):
        for p in range(PIECES):
            at = slice(p * STRIP, (p + 1) * STRIP)
            total = chip_sum[m, chip, at, :].astype(F32)
            for step in range(1, chips):
                to_chip(m, step, p).wait_recv()
                total = total + from_chip[m, step, at, :].astype(F32)
            sums[layer, m, chip, strip(core, p), :] = total.astype(BF16)
            if layer == 0:
                go(to_section(m, p))
            start_spread(layer, m, p)

    def start_spread(layer, m, p):
        for step in range(1, chips):
            go(spread(layer, m, step, p))
        go(share(layer, m, 0, p))

    def relay(m):
        for p in range(PIECES):
            to_section(m, p).wait_recv()
            start_spread(0, m, p)

    def finish_spread(layer, m):
        for p in range(PIECES):
            for step in range(1, chips):
                spread(layer, m, step, p).wait_recv()
                go(share(layer, m, step, p))

    def spread_done(layer, m):
        for p in range(PIECES):
            for step in range(chips):
                share(layer, m, step, p).wait_recv()

    def out_copy(m):
        return pltpu.make_async_copy(result.at[m], out_ref.at[m], out_sem.at[m])

    def add_own(layer, m, source, select_own, target):
        for k in range(chips):
            at = pl.ds(k * cols, cols)
            more = jnp.dot(select_own, sums[layer, m, k], preferred_element_type=F32)
            target[m, :, at] = (source[:, at].astype(F32) + more).astype(BF16)

    def wait_sends():
        for copy in sends:
            copy.wait_send()
        sends.clear()

    @pl.when(sec == 0)
    def _():
        selects = [selection(route_ref, m) for m in range(micro)]
        forward(0)
        forward_other(0)
        gathered(0)
        take(0, selects[0].astype(BF16))
        for copy in weight_copies():
            copy.wait()
        forward(1)
        experts(0, selects[0])
        forward_other(1)
        reduce_core(0)
        gathered(1)
        take(1, selects[1].astype(BF16))
        experts(1, selects[1])
        reduce_chip(0, 0)
        reduce_core(1)
        finish_spread(0, 0)
        reduce_chip(0, 1)
        for m in range(micro):
            if m == 1:
                finish_spread(0, 1)
            spread_done(0, m)
            add_own(0, m, rows.at[m, rows_of(me), :], mine(selects[m].astype(BF16)), result)
            out_copy(m).start()
        route_copy().wait_recv()
        wait_sends()
        for m in range(micro):
            out_copy(m).wait()

    @pl.when(sec == 1)
    def _():
        selects = [selection(route_ref, m) for m in range(micro)]
        for m in range(micro):
            forward(m)
            forward_other(m)
        route_copy().wait_recv()
        before = [selection(peer_route, m).astype(BF16) for m in range(micro)]
        for m in range(micro):
            gathered(m)
            take(m, selects[m].astype(BF16))
        for copy in weight_copies():
            copy.wait()

        def second(m):
            link = dot_nt(selects[m].astype(BF16), before[m]).astype(BF16)
            finish_spread(0, m)
            spread_done(0, m)
            for k in range(chips):
                at = pl.ds(k * cols, cols)
                more = jnp.dot(link, sums[0, m, k], preferred_element_type=F32)
                blocks[m, :, at] = (blocks[m, :, at] + more).astype(BF16).astype(F32)
            experts(m, selects[m])

        def keep(m):
            add_own(0, m, rows.at[m, rows_of(me), :], mine(before[m]), own_rows)

        relay(0)
        second(0)
        reduce_core(0)
        relay(1)
        keep(0)
        second(1)
        reduce_chip(1, 0)
        reduce_core(1)
        keep(1)
        finish_spread(1, 0)
        reduce_chip(1, 1)
        for m in range(micro):
            if m == 1:
                finish_spread(1, 1)
            spread_done(1, m)
            add_own(1, m, own_rows.at[m], mine(selects[m].astype(BF16)), result)
            out_copy(m).start()
        wait_sends()
        for m in range(micro):
            out_copy(m).wait()

    for copy in first:
        copy.wait_send()


def body(tokens_in, norm_gains, w_gate, w_up, w_down, route_ids, route_gates):
    n = lax.axis_size("tensor")
    micro, rpd, width = tokens_in.shape
    chips = n // 2
    cols = width // chips
    tok = n * rpd
    hidden = w_gate.shape[-1]
    picked = route_ids[0] == 0
    chosen = jnp.sum(picked.astype(F32), axis=-1)
    weight = jnp.sum(jnp.where(picked, route_gates[0], 0.0), axis=-1)
    route = jnp.concatenate([chosen, weight, jnp.zeros((8 - 2 * micro, tok), F32)], axis=0)
    dma = pltpu.SemaphoreType.DMA
    out = pl.pallas_call(
        functools.partial(kernel, n, micro),
        out_shape=jax.ShapeDtypeStruct((micro, rpd, width), BF16),
        in_specs=[
            pl.BlockSpec(memory_space=pl.ANY),
            pl.BlockSpec(memory_space=pltpu.VMEM),
            pl.BlockSpec(memory_space=pltpu.VMEM),
            pl.BlockSpec(memory_space=pl.ANY),
            pl.BlockSpec(memory_space=pl.ANY),
            pl.BlockSpec(memory_space=pl.ANY),
        ],
        out_specs=pl.BlockSpec(memory_space=pl.ANY),
        scratch_shapes=[
            pltpu.VMEM((micro, tok, width), BF16),
            pltpu.VMEM((width, hidden), BF16),
            pltpu.VMEM((width, hidden), BF16),
            pltpu.VMEM((hidden, width), BF16),
            pltpu.VMEM((8, tok), F32),
            pltpu.VMEM((micro, CAP, width), F32),
            pltpu.VMEM((micro, chips, CAP, cols), BF16),
            pltpu.VMEM((micro, chips, HALF, cols), BF16),
            pltpu.VMEM((micro, chips, HALF, cols), BF16),
            pltpu.VMEM((micro, chips, HALF, cols), BF16),
            pltpu.VMEM((2, micro, chips, CAP, cols), BF16),
            pltpu.VMEM((micro, rpd, width), BF16),
            pltpu.VMEM((micro, rpd, width), BF16),
            dma((micro,)),
            dma((3,)),
            dma((micro,)),
            dma((2,)),
            dma((micro,)),
            dma((micro,)),
            *[dma((micro, chips, SPLIT)) for _ in range(8)],
            dma((micro,)),
            dma((micro,)),
            dma((micro, chips, PIECES)),
            dma((micro, chips, PIECES)),
            dma((micro, PIECES)),
            dma((micro, PIECES)),
            *[dma((2, micro, chips, PIECES)) for _ in range(4)],
        ],
        compiler_params=pltpu.CompilerParams(
            collective_id=0, has_side_effects=True, vmem_limit_bytes=63 * 1024 * 1024
        ),
        cost_estimate=pl.CostEstimate(flops=2 * 10**9, bytes_accessed=8 * 10**6, transcendentals=10**5),
        name="relay",
    )(tokens_in, norm_gains, route, w_gate[0, 0], w_up[0, 0], w_down[0, 0])
    return out[None]


def solution(mesh):
    return jax.shard_map(
        body,
        mesh=mesh,
        in_specs=(
            P(None, ("dp", "tensor"), None),
            P("section", None),
            P("section", None, None, "tensor"),
            P("section", None, None, "tensor"),
            P("section", None, "tensor", None),
            P("section", None, "dp", None),
            P("section", None, "dp", None),
        ),
        out_specs=P("section", None, ("dp", "tensor"), None),
        check_vma=False,
    )
```

```python
import functools

import jax
import jax.numpy as jnp
from jax import lax
from jax.experimental import pallas as pl
from jax.experimental.pallas import tpu as pltpu
from jax.sharding import PartitionSpec as P

CAP = 128
HALF = CAP // 2
PIECES = 4
STRIP = HALF // PIECES
EVERY = tuple(range(PIECES))
SPLIT = 4
MESH = pl.DeviceIdType.MESH
F32 = jnp.float32
BF16 = jnp.bfloat16


def dot_nt(a, b):
    return lax.dot_general(a, b, (((1,), (1,)), ((), ())), preferred_element_type=F32)


def kernel(
    n, micro, tok_ref, gain_ref, route_ref, wg_hbm, wu_hbm, wd_hbm, out_ref,
    rows, wg, wu, wd, peer_route, blocks, term, from_mate, chip_sum, from_chip, sums, own_rows, result,
    tok_sem, w_sem, out_sem, route_sems,
    g_send, g_recv, y_send, y_recv, x_send, x_recv, fy_send, fy_recv, fx_send, fx_recv, a_send, a_recv, b_send, b_recv, c_send, c_recv, d_send, d_recv, e_send, e_recv,
):
    chips = n // 2
    rpd = tok_ref.shape[1]
    width = tok_ref.shape[2]
    tok = n * rpd
    cols = width // chips
    sec = lax.axis_index("section")
    me = lax.axis_index("tensor")
    chip = me // 2
    core = me % 2
    mate = chip * 2 + (1 - core)
    other = 1 - sec
    sends = []

    def chip_at(step):
        return lax.rem(chip + step, chips)

    def remote(src, dst, send, recv, **where):
        return pltpu.make_async_remote_copy(
            src_ref=src, dst_ref=dst, send_sem=send, recv_sem=recv, device_id=where, device_id_type=MESH
        )

    def rows_of(index):
        return pl.ds(pl.multiple_of(index * rpd, rpd), rpd)

    my_half = pl.ds(pl.multiple_of(core * HALF, HALF), HALF)
    mate_half = pl.ds(pl.multiple_of((1 - core) * HALF, HALF), HALF)

    def own_copy(m):
        return pltpu.make_async_copy(tok_ref.at[m], rows.at[m, rows_of(me), :], tok_sem.at[m])

    def weight_copies():
        pairs = ((wg_hbm, wg), (wu_hbm, wu), (wd_hbm, wd))
        return [pltpu.make_async_copy(src, dst, w_sem.at[i]) for i, (src, dst) in enumerate(pairs)]

    for m in range(micro):
        own_copy(m).start()
    for copy in weight_copies():
        copy.start()

    barrier = pltpu.get_barrier_semaphore()
    for step in range(1, chips):
        pl.semaphore_signal(barrier, inc=1, device_id={"tensor": chip_at(step) * 2 + core}, device_id_type=MESH)
    pl.semaphore_signal(barrier, inc=1, device_id={"tensor": mate}, device_id_type=MESH)
    pl.semaphore_signal(barrier, inc=1, device_id={"section": other}, device_id_type=MESH)
    pl.semaphore_wait(barrier, chips + 1)

    span = width // 2 // SPLIT

    def route_copy():
        return remote(route_ref, peer_route, route_sems.at[0], route_sems.at[1], section=other)

    def lanes_of(section, i):
        return pl.ds(pl.multiple_of(section * (width // 2) + i * span, 128), span)

    def own_to_mate(m):
        return remote(tok_ref.at[m], rows.at[m, rows_of(me), :], g_send.at[m], g_recv.at[m], tensor=mate)

    def over_chips(m, step, i):
        lanes = lanes_of(sec, i)
        return remote(
            tok_ref.at[m, :, lanes], rows.at[m, rows_of(me), lanes], y_send.at[m, step, i], y_recv.at[m, step, i],
            tensor=chip_at(step) * 2 + core,
        )

    def from_step(step):
        return chip_at(chips - step) * 2 + core

    def over_sections(m, step, i):
        place = rows.at[m, rows_of(from_step(step)), lanes_of(sec, i)]
        return remote(place, place, x_send.at[m, step, i], x_recv.at[m, step, i], section=other)

    def pass_own(m, step, i):
        place = rows.at[m, rows_of(from_step(step)), lanes_of(sec, i)]
        return remote(place, place, fy_send.at[m, step, i], fy_recv.at[m, step, i], tensor=mate)

    def pass_other(m, step, i):
        place = rows.at[m, rows_of(from_step(step)), lanes_of(other, i)]
        return remote(place, place, fx_send.at[m, step, i], fx_recv.at[m, step, i], tensor=mate)

    hops = [(step, i) for i in range(SPLIT) for step in range(1, chips)]
    first = []
    for m in range(micro):
        for step, i in hops:
            over_chips(m, step, i).start()
            first.append(over_chips(m, step, i))
        own_to_mate(m).start()
        first.append(own_to_mate(m))
        if m == 0:
            route_copy().start()
            first.append(route_copy())

    def forward(m, i):
        for step in range(1, chips):
            over_chips(m, step, i).wait_recv()
            go(over_sections(m, step, i))
            go(pass_own(m, step, i))

    def forward_other(m, i):
        for step in range(1, chips):
            over_sections(m, step, i).wait_recv()
            go(pass_other(m, step, i))

    def forward_rows():
        lag = max(1, SPLIT - 1)
        count = micro * SPLIT
        for at in range(count):
            forward(at // SPLIT, at % SPLIT)
            if at >= lag:
                forward_other((at - lag) // SPLIT, (at - lag) % SPLIT)
        return [((at) // SPLIT, at % SPLIT) for at in range(count - lag, count)]

    def gathered(m):
        own_copy(m).wait()
        own_to_mate(m).wait_recv()
        for step, i in hops:
            pass_own(m, step, i).wait_recv()
            pass_other(m, step, i).wait_recv()

    tri = (
        lax.broadcasted_iota(jnp.int32, (tok, tok), 0) <= lax.broadcasted_iota(jnp.int32, (tok, tok), 1)
    ).astype(F32).astype(BF16)

    def selection(ref, m):
        chosen = ref[m : m + 1, :]
        counts = jnp.dot(jnp.broadcast_to(chosen, (16, tok)).astype(BF16), tri, preferred_element_type=F32)
        slot = (counts[0:1, :] - 1.0).astype(jnp.int32)
        hit = (slot == lax.broadcasted_iota(jnp.int32, (CAP, tok), 0)) & (chosen > 0.5)
        return jnp.where(hit, 1.0, 0.0)

    def mine(select):
        pick = lax.broadcasted_iota(jnp.int32, (rpd, tok), 1) == lax.broadcasted_iota(
            jnp.int32, (rpd, tok), 0
        ) + me * rpd
        return dot_nt(pick.astype(F32).astype(BF16), select).astype(BF16)

    def take(m, select):
        for k in range(chips):
            at = pl.ds(k * cols, cols)
            blocks[m, :, at] = jnp.dot(select, rows[m, :, at], preferred_element_type=F32)

    def experts(m, select):
        weight = jnp.sum(select * route_ref[micro + m : micro + m + 1, :], axis=1, keepdims=True)
        block = blocks[m]
        scale = lax.rsqrt(jnp.mean(block * block, axis=1, keepdims=True) + 1e-05)
        normed = (block * scale * gain_ref[...]).astype(BF16)
        gate = jnp.dot(normed, wg[...], preferred_element_type=F32)
        up = jnp.dot(normed, wu[...], preferred_element_type=F32)
        act = (gate / (1.0 + jnp.exp(-gate)) * up).astype(BF16)
        for k in range(chips):
            part = jnp.dot(act, wd[:, k * cols : (k + 1) * cols], preferred_element_type=F32)
            term[m, k] = (part * weight).astype(BF16)
        copy = to_mate(m)
        copy.start()
        sends.append(copy)

    def to_mate(m):
        return remote(term.at[m, :, mate_half, :], from_mate.at[m], a_send.at[m], a_recv.at[m], tensor=mate)

    def strip(base, p):
        return pl.ds(pl.multiple_of(base * HALF + p * STRIP, STRIP), STRIP)

    def to_chip(m, step, p):
        there = chip_at(step)
        at = pl.ds(p * STRIP, STRIP)
        return remote(
            chip_sum.at[m, there, at, :], from_chip.at[m, step, at, :], b_send.at[m, step, p], b_recv.at[m, step, p],
            tensor=there * 2 + core,
        )

    def to_section(m, step, p):
        place = sums.at[0, m, chip_at(chips - step), strip(core, p), :]
        return remote(place, place, c_send.at[m, step, p], c_recv.at[m, step, p], section=other)

    def spread(layer, m, step, p):
        place = sums.at[layer, m, chip, strip(core, p), :]
        return remote(
            place, place, d_send.at[layer, m, step, p], d_recv.at[layer, m, step, p], tensor=chip_at(step) * 2 + core
        )

    def share(layer, m, step, p):
        place = sums.at[layer, m, chip_at(chips - step), strip(core, p), :]
        return remote(place, place, e_send.at[layer, m, step, p], e_recv.at[layer, m, step, p], tensor=mate)

    def go(copy):
        copy.start()
        sends.append(copy)

    def reduce_core(m):
        to_mate(m).wait_recv()
        for k in range(chips):
            chip_sum[m, k] = (term[m, k, my_half, :].astype(F32) + from_mate[m, k].astype(F32)).astype(BF16)
        for p in range(PIECES):
            for step in range(1, chips):
                go(to_chip(m, step, p))

    def reduce_chip(layer, m):
        for p in EVERY:
            at = slice(p * STRIP, (p + 1) * STRIP)
            total = chip_sum[m, chip, at, :].astype(F32)
            for step in range(1, chips):
                to_chip(m, step, p).wait_recv()
                total = total + from_chip[m, step, at, :].astype(F32)
            sums[layer, m, chip, strip(core, p), :] = total.astype(BF16)
            if layer == 0:
                go(to_section(m, 0, p))
            start_spread(layer, m, p)

    def start_spread(layer, m, p):
        for step in range(1, chips):
            go(spread(layer, m, step, p))
        go(share(layer, m, 0, p))

    def relay(m, steps):
        for step in steps:
            for p in EVERY:
                to_section(m, step, p).wait_recv()
                go(share(0, m, step, p))

    def finish_spread(layer, m):
        for p in EVERY:
            for step in range(1, chips):
                spread(layer, m, step, p).wait_recv()
                if layer == 0:
                    go(to_section(m, step, p))
                go(share(layer, m, step, p))

    def spread_done(layer, m):
        for p in range(PIECES):
            for step in range(chips):
                share(layer, m, step, p).wait_recv()

    def out_copy(m):
        return pltpu.make_async_copy(result.at[m], out_ref.at[m], out_sem.at[m])

    def add_own(layer, m, source, select_own, target):
        for k in range(chips):
            at = pl.ds(k * cols, cols)
            more = jnp.dot(select_own, sums[layer, m, k], preferred_element_type=F32)
            target[m, :, at] = (source[:, at].astype(F32) + more).astype(BF16)

    def wait_sends():
        for copy in sends:
            copy.wait_send()
        sends.clear()

    @pl.when(sec == 0)
    def _():
        selects = [selection(route_ref, m) for m in range(micro)]
        left = forward_rows()
        gathered(0)
        take(0, selects[0].astype(BF16))
        for copy in weight_copies():
            copy.wait()
        experts(0, selects[0])
        for m, i in left:
            forward_other(m, i)
        reduce_core(0)
        gathered(1)
        take(1, selects[1].astype(BF16))
        experts(1, selects[1])
        reduce_chip(0, 0)
        reduce_core(1)
        finish_spread(0, 0)
        reduce_chip(0, 1)
        for m in range(micro):
            if m == 1:
                finish_spread(0, 1)
            spread_done(0, m)
            add_own(0, m, rows.at[m, rows_of(me), :], mine(selects[m].astype(BF16)), result)
            out_copy(m).start()
        route_copy().wait_recv()
        wait_sends()
        for m in range(micro):
            out_copy(m).wait()

    @pl.when(sec == 1)
    def _():
        selects = [selection(route_ref, m) for m in range(micro)]
        for m, i in forward_rows():
            forward_other(m, i)
        route_copy().wait_recv()
        before = [selection(peer_route, m).astype(BF16) for m in range(micro)]
        for m in range(micro):
            gathered(m)
            take(m, selects[m].astype(BF16))
        for copy in weight_copies():
            copy.wait()

        def second(m):
            link = dot_nt(selects[m].astype(BF16), before[m]).astype(BF16)
            spread_done(0, m)
            for k in range(chips):
                at = pl.ds(k * cols, cols)
                more = jnp.dot(link, sums[0, m, k], preferred_element_type=F32)
                blocks[m, :, at] = (blocks[m, :, at] + more).astype(BF16).astype(F32)
            experts(m, selects[m])

        def keep(m):
            add_own(0, m, rows.at[m, rows_of(me), :], mine(before[m]), own_rows)

        def finish(m):
            finish_spread(1, m)
            spread_done(1, m)
            add_own(1, m, own_rows.at[m], mine(selects[m].astype(BF16)), result)
            out_copy(m).start()

        relay(0, range(chips))
        second(0)
        reduce_core(0)
        keep(0)
        relay(1, range(1))
        reduce_chip(1, 0)
        relay(1, range(1, chips))
        second(1)
        reduce_core(1)
        keep(1)
        finish(0)
        reduce_chip(1, 1)
        finish(1)
        wait_sends()
        for m in range(micro):
            out_copy(m).wait()

    for copy in first:
        copy.wait_send()


def body(tokens_in, norm_gains, w_gate, w_up, w_down, route_ids, route_gates):
    n = lax.axis_size("tensor")
    micro, rpd, width = tokens_in.shape
    chips = n // 2
    cols = width // chips
    tok = n * rpd
    hidden = w_gate.shape[-1]
    picked = route_ids[0] == 0
    chosen = jnp.sum(picked.astype(F32), axis=-1)
    weight = jnp.sum(jnp.where(picked, route_gates[0], 0.0), axis=-1)
    route = jnp.concatenate([chosen, weight, jnp.zeros((8 - 2 * micro, tok), F32)], axis=0)
    dma = pltpu.SemaphoreType.DMA
    out = pl.pallas_call(
        functools.partial(kernel, n, micro),
        out_shape=jax.ShapeDtypeStruct((micro, rpd, width), BF16),
        in_specs=[
            pl.BlockSpec(memory_space=pl.ANY),
            pl.BlockSpec(memory_space=pltpu.VMEM),
            pl.BlockSpec(memory_space=pltpu.VMEM),
            pl.BlockSpec(memory_space=pl.ANY),
            pl.BlockSpec(memory_space=pl.ANY),
            pl.BlockSpec(memory_space=pl.ANY),
        ],
        out_specs=pl.BlockSpec(memory_space=pl.ANY),
        scratch_shapes=[
            pltpu.VMEM((micro, tok, width), BF16),
            pltpu.VMEM((width, hidden), BF16),
            pltpu.VMEM((width, hidden), BF16),
            pltpu.VMEM((hidden, width), BF16),
            pltpu.VMEM((8, tok), F32),
            pltpu.VMEM((micro, CAP, width), F32),
            pltpu.VMEM((micro, chips, CAP, cols), BF16),
            pltpu.VMEM((micro, chips, HALF, cols), BF16),
            pltpu.VMEM((micro, chips, HALF, cols), BF16),
            pltpu.VMEM((micro, chips, HALF, cols), BF16),
            pltpu.VMEM((2, micro, chips, CAP, cols), BF16),
            pltpu.VMEM((micro, rpd, width), BF16),
            pltpu.VMEM((micro, rpd, width), BF16),
            dma((micro,)),
            dma((3,)),
            dma((micro,)),
            dma((2,)),
            dma((micro,)),
            dma((micro,)),
            *[dma((micro, chips, SPLIT)) for _ in range(8)],
            dma((micro,)),
            dma((micro,)),
            dma((micro, chips, PIECES)),
            dma((micro, chips, PIECES)),
            dma((micro, chips, PIECES)),
            dma((micro, chips, PIECES)),
            *[dma((2, micro, chips, PIECES)) for _ in range(4)],
        ],
        compiler_params=pltpu.CompilerParams(
            collective_id=0, has_side_effects=True, vmem_limit_bytes=63 * 1024 * 1024
        ),
        cost_estimate=pl.CostEstimate(flops=2 * 10**9, bytes_accessed=8 * 10**6, transcendentals=10**5),
        name="relay",
    )(tokens_in, norm_gains, route, w_gate[0, 0], w_up[0, 0], w_down[0, 0])
    return out[None]


def solution(mesh):
    return jax.shard_map(
        body,
        mesh=mesh,
        in_specs=(
            P(None, ("dp", "tensor"), None),
            P("section", None),
            P("section", None, None, "tensor"),
            P("section", None, None, "tensor"),
            P("section", None, "tensor", None),
            P("section", None, "dp", None),
            P("section", None, "dp", None),
        ),
        out_specs=P("section", None, ("dp", "tensor"), None),
        check_vma=False,
    )
```

```python
import functools

import jax
import jax.numpy as jnp
from jax import lax
from jax.experimental import pallas as pl
from jax.experimental.pallas import tpu as pltpu
from jax.sharding import PartitionSpec as P

CAP = 128
HALF = CAP // 2
PIECES = 4
STRIP = HALF // PIECES
EVERY = tuple(range(PIECES))
SPLIT = 4
MESH = pl.DeviceIdType.MESH
F32 = jnp.float32
BF16 = jnp.bfloat16


def dot_nt(a, b):
    return lax.dot_general(a, b, (((1,), (1,)), ((), ())), preferred_element_type=F32)


def kernel(
    n, micro, tok_ref, gain_ref, route_ref, wg_hbm, wu_hbm, wd_hbm, out_ref,
    rows, wg, wu, wd, peer_route, blocks, term, from_mate, chip_sum, from_chip, sums, own_rows, result,
    tok_sem, w_sem, out_sem, route_sems,
    g_send, g_recv, y_send, y_recv, x_send, x_recv, fy_send, fy_recv, fx_send, fx_recv, a_send, a_recv, b_send, b_recv, c_send, c_recv, d_send, d_recv, e_send, e_recv,
):
    chips = n // 2
    rpd = tok_ref.shape[1]
    width = tok_ref.shape[2]
    tok = n * rpd
    cols = width // chips
    sec = lax.axis_index("section")
    me = lax.axis_index("tensor")
    chip = me // 2
    core = me % 2
    mate = chip * 2 + (1 - core)
    other = 1 - sec
    sends = []

    def chip_at(step):
        return lax.rem(chip + step, chips)

    def remote(src, dst, send, recv, **where):
        return pltpu.make_async_remote_copy(
            src_ref=src, dst_ref=dst, send_sem=send, recv_sem=recv, device_id=where, device_id_type=MESH
        )

    def rows_of(index):
        return pl.ds(pl.multiple_of(index * rpd, rpd), rpd)

    my_half = pl.ds(pl.multiple_of(core * HALF, HALF), HALF)
    mate_half = pl.ds(pl.multiple_of((1 - core) * HALF, HALF), HALF)

    def own_copy(m):
        return pltpu.make_async_copy(tok_ref.at[m], rows.at[m, rows_of(me), :], tok_sem.at[m])

    def weight_copies():
        pairs = ((wg_hbm, wg), (wu_hbm, wu), (wd_hbm, wd))
        return [pltpu.make_async_copy(src, dst, w_sem.at[i]) for i, (src, dst) in enumerate(pairs)]

    for m in range(micro):
        own_copy(m).start()
    for copy in weight_copies():
        copy.start()

    barrier = pltpu.get_barrier_semaphore()
    for step in range(1, chips):
        pl.semaphore_signal(barrier, inc=1, device_id={"tensor": chip_at(step) * 2 + core}, device_id_type=MESH)
    pl.semaphore_signal(barrier, inc=1, device_id={"tensor": mate}, device_id_type=MESH)
    pl.semaphore_signal(barrier, inc=1, device_id={"section": other}, device_id_type=MESH)
    pl.semaphore_wait(barrier, chips + 1)

    span = width // 2 // SPLIT

    def route_copy():
        return remote(route_ref, peer_route, route_sems.at[0], route_sems.at[1], section=other)

    def lanes_of(section, i):
        return pl.ds(pl.multiple_of(section * (width // 2) + i * span, 128), span)

    def own_to_mate(m):
        return remote(tok_ref.at[m], rows.at[m, rows_of(me), :], g_send.at[m], g_recv.at[m], tensor=mate)

    def over_chips(m, step, i):
        lanes = lanes_of(sec, i)
        return remote(
            tok_ref.at[m, :, lanes], rows.at[m, rows_of(me), lanes], y_send.at[m, step, i], y_recv.at[m, step, i],
            tensor=chip_at(step) * 2 + core,
        )

    def from_step(step):
        return chip_at(chips - step) * 2 + core

    def over_sections(m, step, i):
        place = rows.at[m, rows_of(from_step(step)), lanes_of(sec, i)]
        return remote(place, place, x_send.at[m, step, i], x_recv.at[m, step, i], section=other)

    def pass_own(m, step, i):
        place = rows.at[m, rows_of(from_step(step)), lanes_of(sec, i)]
        return remote(place, place, fy_send.at[m, step, i], fy_recv.at[m, step, i], tensor=mate)

    def pass_other(m, step, i):
        place = rows.at[m, rows_of(from_step(step)), lanes_of(other, i)]
        return remote(place, place, fx_send.at[m, step, i], fx_recv.at[m, step, i], tensor=mate)

    hops = [(step, i) for i in range(SPLIT) for step in range(1, chips)]
    first = []
    for m in range(micro):
        for step, i in hops:
            over_chips(m, step, i).start()
            first.append(over_chips(m, step, i))
        own_to_mate(m).start()
        first.append(own_to_mate(m))
        if m == 0:
            route_copy().start()
            first.append(route_copy())

    def forward(m, i):
        for step in range(1, chips):
            over_chips(m, step, i).wait_recv()
            go(over_sections(m, step, i))
            go(pass_own(m, step, i))

    def forward_other(m, i):
        for step in range(1, chips):
            over_sections(m, step, i).wait_recv()
            go(pass_other(m, step, i))

    def forward_rows():
        lag = max(1, SPLIT - 1)
        count = micro * SPLIT
        for at in range(count):
            forward(at // SPLIT, at % SPLIT)
            if at >= lag:
                forward_other((at - lag) // SPLIT, (at - lag) % SPLIT)
        return [((at) // SPLIT, at % SPLIT) for at in range(count - lag, count)]

    def gathered(m):
        own_copy(m).wait()
        own_to_mate(m).wait_recv()
        for step, i in hops:
            pass_own(m, step, i).wait_recv()
            pass_other(m, step, i).wait_recv()

    tri = (
        lax.broadcasted_iota(jnp.int32, (tok, tok), 0) <= lax.broadcasted_iota(jnp.int32, (tok, tok), 1)
    ).astype(F32).astype(BF16)

    def selection(ref, m):
        chosen = ref[m : m + 1, :]
        counts = jnp.dot(jnp.broadcast_to(chosen, (16, tok)).astype(BF16), tri, preferred_element_type=F32)
        slot = (counts[0:1, :] - 1.0).astype(jnp.int32)
        hit = (slot == lax.broadcasted_iota(jnp.int32, (CAP, tok), 0)) & (chosen > 0.5)
        return jnp.where(hit, 1.0, 0.0)

    def mine(select):
        pick = lax.broadcasted_iota(jnp.int32, (rpd, tok), 1) == lax.broadcasted_iota(
            jnp.int32, (rpd, tok), 0
        ) + me * rpd
        return dot_nt(pick.astype(F32).astype(BF16), select).astype(BF16)

    def take(m, select):
        for k in range(chips):
            at = pl.ds(k * cols, cols)
            blocks[m, :, at] = jnp.dot(select, rows[m, :, at], preferred_element_type=F32)

    def experts(m, select):
        weight = jnp.sum(select * route_ref[micro + m : micro + m + 1, :], axis=1, keepdims=True)
        block = blocks[m]
        scale = lax.rsqrt(jnp.mean(block * block, axis=1, keepdims=True) + 1e-05)
        normed = (block * scale * gain_ref[...]).astype(BF16)
        gate = jnp.dot(normed, wg[...], preferred_element_type=F32)
        up = jnp.dot(normed, wu[...], preferred_element_type=F32)
        act = (gate / (1.0 + jnp.exp(-gate)) * up).astype(BF16)
        for k in range(chips):
            part = jnp.dot(act, wd[:, k * cols : (k + 1) * cols], preferred_element_type=F32)
            term[m, k] = (part * weight).astype(BF16)
        copy = to_mate(m)
        copy.start()
        sends.append(copy)

    def to_mate(m):
        return remote(term.at[m, :, mate_half, :], from_mate.at[m], a_send.at[m], a_recv.at[m], tensor=mate)

    def strip(base, p):
        return pl.ds(pl.multiple_of(base * HALF + p * STRIP, STRIP), STRIP)

    def to_chip(m, step, p):
        there = chip_at(step)
        at = pl.ds(p * STRIP, STRIP)
        return remote(
            chip_sum.at[m, there, at, :], from_chip.at[m, step, at, :], b_send.at[m, step, p], b_recv.at[m, step, p],
            tensor=there * 2 + core,
        )

    def to_section(m, step, p):
        place = sums.at[0, m, chip_at(chips - step), strip(core, p), :]
        return remote(place, place, c_send.at[m, step, p], c_recv.at[m, step, p], section=other)

    def spread(layer, m, step, p):
        place = sums.at[layer, m, chip, strip(core, p), :]
        return remote(
            place, place, d_send.at[layer, m, step, p], d_recv.at[layer, m, step, p], tensor=chip_at(step) * 2 + core
        )

    def share(layer, m, step, p):
        place = sums.at[layer, m, chip_at(chips - step), strip(core, p), :]
        return remote(place, place, e_send.at[layer, m, step, p], e_recv.at[layer, m, step, p], tensor=mate)

    def go(copy):
        copy.start()
        sends.append(copy)

    def reduce_core(m):
        to_mate(m).wait_recv()
        for k in range(chips):
            chip_sum[m, k] = (term[m, k, my_half, :].astype(F32) + from_mate[m, k].astype(F32)).astype(BF16)
        for p in range(PIECES):
            for step in range(1, chips):
                go(to_chip(m, step, p))

    def reduce_chip(layer, m):
        for p in EVERY:
            at = slice(p * STRIP, (p + 1) * STRIP)
            total = chip_sum[m, chip, at, :].astype(F32)
            for step in range(1, chips):
                to_chip(m, step, p).wait_recv()
                total = total + from_chip[m, step, at, :].astype(F32)
            sums[layer, m, chip, strip(core, p), :] = total.astype(BF16)
            if layer == 0:
                go(to_section(m, 0, p))
            start_spread(layer, m, p)

    def start_spread(layer, m, p):
        for step in range(1, chips):
            go(spread(layer, m, step, p))
        go(share(layer, m, 0, p))

    def relay(m, steps):
        for step in steps:
            for p in EVERY:
                to_section(m, step, p).wait_recv()
                go(share(0, m, step, p))

    def finish_spread(layer, m):
        for p in EVERY:
            for step in range(1, chips):
                spread(layer, m, step, p).wait_recv()
                if layer == 0:
                    go(to_section(m, step, p))
                go(share(layer, m, step, p))

    def spread_done(layer, m):
        for p in range(PIECES):
            for step in range(chips):
                share(layer, m, step, p).wait_recv()

    def out_copy(m):
        return pltpu.make_async_copy(result.at[m], out_ref.at[m], out_sem.at[m])

    def add_own(layer, m, source, select_own, target):
        for k in range(chips):
            at = pl.ds(k * cols, cols)
            more = jnp.dot(select_own, sums[layer, m, k], preferred_element_type=F32)
            target[m, :, at] = (source[:, at].astype(F32) + more).astype(BF16)

    def wait_sends():
        for copy in sends:
            copy.wait_send()
        sends.clear()

    @pl.when(sec == 0)
    def _():
        selects = [selection(route_ref, m) for m in range(micro)]
        left = forward_rows()
        gathered(0)
        take(0, selects[0].astype(BF16))
        for copy in weight_copies():
            copy.wait()
        experts(0, selects[0])
        for m, i in left:
            forward_other(m, i)
        reduce_core(0)
        gathered(1)
        take(1, selects[1].astype(BF16))
        experts(1, selects[1])
        reduce_chip(0, 0)
        reduce_core(1)
        finish_spread(0, 0)
        reduce_chip(0, 1)
        finish_spread(0, 1)
        for m in range(micro):
            spread_done(0, m)
            add_own(0, m, rows.at[m, rows_of(me), :], mine(selects[m].astype(BF16)), result)
            out_copy(m).start()
        route_copy().wait_recv()
        wait_sends()
        for m in range(micro):
            out_copy(m).wait()

    @pl.when(sec == 1)
    def _():
        selects = [selection(route_ref, m) for m in range(micro)]
        for m, i in forward_rows():
            forward_other(m, i)
        route_copy().wait_recv()
        before = [selection(peer_route, m).astype(BF16) for m in range(micro)]
        for m in range(micro):
            gathered(m)
            take(m, selects[m].astype(BF16))
        for copy in weight_copies():
            copy.wait()

        def second(m):
            link = dot_nt(selects[m].astype(BF16), before[m]).astype(BF16)
            spread_done(0, m)
            for k in range(chips):
                at = pl.ds(k * cols, cols)
                more = jnp.dot(link, sums[0, m, k], preferred_element_type=F32)
                blocks[m, :, at] = (blocks[m, :, at] + more).astype(BF16).astype(F32)
            experts(m, selects[m])

        def keep(m):
            add_own(0, m, rows.at[m, rows_of(me), :], mine(before[m]), own_rows)

        def finish(m):
            finish_spread(1, m)
            spread_done(1, m)
            add_own(1, m, own_rows.at[m], mine(selects[m].astype(BF16)), result)
            out_copy(m).start()

        relay(0, range(chips))
        second(0)
        reduce_core(0)
        keep(0)
        relay(1, range(1))
        reduce_chip(1, 0)
        relay(1, range(1, chips))
        second(1)
        reduce_core(1)
        keep(1)
        finish(0)
        reduce_chip(1, 1)
        finish(1)
        wait_sends()
        for m in range(micro):
            out_copy(m).wait()

    for copy in first:
        copy.wait_send()


def body(tokens_in, norm_gains, w_gate, w_up, w_down, route_ids, route_gates):
    n = lax.axis_size("tensor")
    micro, rpd, width = tokens_in.shape
    chips = n // 2
    cols = width // chips
    tok = n * rpd
    hidden = w_gate.shape[-1]
    picked = route_ids[0] == 0
    chosen = jnp.sum(picked.astype(F32), axis=-1)
    weight = jnp.sum(jnp.where(picked, route_gates[0], 0.0), axis=-1)
    route = jnp.concatenate([chosen, weight, jnp.zeros((8 - 2 * micro, tok), F32)], axis=0)
    dma = pltpu.SemaphoreType.DMA
    out = pl.pallas_call(
        functools.partial(kernel, n, micro),
        out_shape=jax.ShapeDtypeStruct((micro, rpd, width), BF16),
        in_specs=[
            pl.BlockSpec(memory_space=pl.ANY),
            pl.BlockSpec(memory_space=pltpu.VMEM),
            pl.BlockSpec(memory_space=pltpu.VMEM),
            pl.BlockSpec(memory_space=pl.ANY),
            pl.BlockSpec(memory_space=pl.ANY),
            pl.BlockSpec(memory_space=pl.ANY),
        ],
        out_specs=pl.BlockSpec(memory_space=pl.ANY),
        scratch_shapes=[
            pltpu.VMEM((micro, tok, width), BF16),
            pltpu.VMEM((width, hidden), BF16),
            pltpu.VMEM((width, hidden), BF16),
            pltpu.VMEM((hidden, width), BF16),
            pltpu.VMEM((8, tok), F32),
            pltpu.VMEM((micro, CAP, width), F32),
            pltpu.VMEM((micro, chips, CAP, cols), BF16),
            pltpu.VMEM((micro, chips, HALF, cols), BF16),
            pltpu.VMEM((micro, chips, HALF, cols), BF16),
            pltpu.VMEM((micro, chips, HALF, cols), BF16),
            pltpu.VMEM((2, micro, chips, CAP, cols), BF16),
            pltpu.VMEM((micro, rpd, width), BF16),
            pltpu.VMEM((micro, rpd, width), BF16),
            dma((micro,)),
            dma((3,)),
            dma((micro,)),
            dma((2,)),
            dma((micro,)),
            dma((micro,)),
            *[dma((micro, chips, SPLIT)) for _ in range(8)],
            dma((micro,)),
            dma((micro,)),
            dma((micro, chips, PIECES)),
            dma((micro, chips, PIECES)),
            dma((micro, chips, PIECES)),
            dma((micro, chips, PIECES)),
            *[dma((2, micro, chips, PIECES)) for _ in range(4)],
        ],
        compiler_params=pltpu.CompilerParams(
            collective_id=0, has_side_effects=True, vmem_limit_bytes=63 * 1024 * 1024
        ),
        cost_estimate=pl.CostEstimate(flops=2 * 10**9, bytes_accessed=8 * 10**6, transcendentals=10**5),
        name="relay",
    )(tokens_in, norm_gains, route, w_gate[0, 0], w_up[0, 0], w_down[0, 0])
    return out[None]


def solution(mesh):
    return jax.shard_map(
        body,
        mesh=mesh,
        in_specs=(
            P(None, ("dp", "tensor"), None),
            P("section", None),
            P("section", None, None, "tensor"),
            P("section", None, None, "tensor"),
            P("section", None, "tensor", None),
            P("section", None, "dp", None),
            P("section", None, "dp", None),
        ),
        out_specs=P("section", None, ("dp", "tensor"), None),
        check_vma=False,
    )
```
